32 devices in a mesh: tm: 8 (over z, x), panel: 4 (over y, core).
Axes of the slice: x: 2, y: 2, z: 4, core: 2. Of those that a mesh axis runs over, the one named last changes fastest.
Arguments:
- spins: int32 [8, 1152], P('tm'), may hold values from -1 to 1, as said below
- neighbours: int32 [1152, 4], replicated, may hold values from 0 to 1151, as said below
- start: float32 [9216, 1152], P(('tm', 'panel')), may hold values from -6 to 6
Outputs:
- panels: float32 [9216, 1152], P(('tm', 'panel'))
- growth: float32 [9216], P(('tm', 'panel'))
The draws below stay inside these ranges and needn't reach their ends.
Inputs may be any that keep to these rules, and one draw needn't show every extreme that they name: `spins`: each entry is -1 or +1. The nearest neighbours of a periodic (24) x 48 square lattice whose sites carry a random labelling; the table is symmetric.
All inputs are finite; a program needn't handle non-finite values.
Results may differ from the reference program's by a relative error of at most 0.0092.
Values may be sent and summed in bfloat16 or wider, within the bound.
A program may use at most 64 MiB of HBM per device.

```python
import jax
import jax.numpy as jnp
from jax import lax

N = 1152
SLICES = 8
STEPS = 4


def draw_spins(key, part):
    values = jax.random.randint(key, (SLICES, N), 0, 2)
    return (2 * values - 1).astype(jnp.int32)


def draw_neighbours(key, part):
    order = jax.random.permutation(key, N).astype(jnp.int32)
    place = jnp.arange(N, dtype=jnp.int32)
    height = N // 48
    line = place // 48
    column = place % 48
    beside = jnp.stack([(line + 1) % height * 48 + column, (line + height - 1) % height * 48 + column, line * 48 + (column + 1) % 48, line * 48 + (column + 47) % 48], axis=1)
    table = jnp.zeros((N, 4), jnp.int32).at[order].set(order[beside])
    return table.astype(jnp.int32)


def levels(stream_key, shape, pieces, smallest, top_value):
    def one(dim, shards_of):
        heights = jax.random.uniform(jax.random.fold_in(jax.random.fold_in(stream_key, 6), dim), (shards_of,), jnp.float32, smallest / len(pieces), top_value / len(pieces))
        return jnp.repeat(jnp.exp(heights), shape[dim] // shards_of).reshape((-1,) + (1,) * (len(shape) - dim - 1))

    loudness = one(*pieces[0])
    for cut in pieces[1:]:
        loudness = loudness * one(*cut)
    return loudness


def bell_draw(rng, extent, scale, most, cuts=(), held_as=jnp.bfloat16):
    values = jax.random.normal(rng, extent, jnp.float32) * scale
    if len(cuts) > 0:
        values = levels(rng, extent, cuts, -0.22, 0.18) * values
    return jnp.clip(values, min=-most, max=most).astype(held_as)


def setup_inputs(seed: int = 0) -> dict:
    key_of = jax.random.split(jax.random.key(seed), 4)
    return {
        "spins": draw_spins(jax.random.fold_in(key_of[3], 71), 0),
        "neighbours": draw_neighbours(jax.random.fold_in(key_of[3], 71), 0),
        "start": bell_draw(key_of[2], (SLICES * N, N), 1.0, 6.0, ((0, 32),), jnp.float32),
    }


DTAU = 0.0625
LAMBDA = 0.5
EPS = 1e-06

def build_hop(neighbours):
    labels = jnp.arange(N, dtype=jnp.int32)
    kmat = jnp.zeros((N, N), jnp.float32)
    for k in range(4):
        kmat = kmat + (neighbours[:, k][:, None] == labels[None, :]).astype(jnp.float32)
    ksq = jnp.dot(kmat, kmat, precision=lax.Precision.HIGHEST)
    eye = jnp.eye(N, dtype=jnp.float32)
    return (eye + DTAU * kmat + 0.5 * DTAU * DTAU * ksq).astype(jnp.bfloat16)

def apply_all(stack, hop, factor):
    prod = jnp.einsum('lij,jk->lik', stack.astype(jnp.float32), hop.astype(jnp.float32), precision=lax.Precision.HIGHEST)
    return (prod * factor[:, None, :]).astype(jnp.bfloat16)

def reference(spins, neighbours, start):
    hop = build_hop(neighbours)
    factor = jnp.exp(LAMBDA * spins.astype(jnp.float32))
    single = (hop.astype(jnp.float32)[None, :, :] * factor[:, None, :]).astype(jnp.bfloat16)
    pair = apply_all(jnp.roll(single, 1, axis=0), hop, factor)
    triple = apply_all(jnp.roll(pair, 1, axis=0), hop, factor)
    block = apply_all(jnp.roll(triple, 1, axis=0), hop, factor)
    current = start.reshape(SLICES, N, N)
    sign = jnp.where(jnp.arange(SLICES) < 4, -1.0, 1.0).astype(jnp.float32)
    logsum = jnp.zeros((SLICES, N), jnp.float32)
    for step in range(STEPS):
        rounded = jnp.roll(current.astype(jnp.bfloat16), 4, axis=0)
        image = jnp.einsum('lij,ljk->lik', rounded.astype(jnp.float32), block.astype(jnp.float32), precision=lax.Precision.HIGHEST)
        image = image * sign[:, None, None]
        rms = jnp.sqrt(lax.optimization_barrier(jnp.mean(image * image, axis=2)) + EPS)
        current = image / rms[:, :, None]
        logsum = logsum + jnp.log(rms)
    return (current.reshape(SLICES * N, N), (logsum / (4.0 * STEPS)).reshape(SLICES * N))
```

```python
import functools

import jax
import jax.numpy as jnp
from jax import lax
from jax.experimental import pallas as pl
from jax.experimental.pallas import tpu as pltpu
from jax.sharding import PartitionSpec as P

STEPS = 4
SPAN = 4
DTAU = 0.0625
LAMBDA = 0.5
EPS = 1e-06
TILE = 256
MESH = pl.DeviceIdType.MESH


def column_tiles(sites):
    return [(at, min(TILE, sites - at)) for at in range(0, sites, TILE)]


def kernel(
    slices, spins_ref, table_ref, start_ref, panels_ref, growth_ref,
    spins_all, factors, bonds, bonds8, rest, now, held, squares, logs, landed, scale_row,
    start_sem, spin_send, spin_recv, log_send, log_recv,
):
    rows, sites = now.shape
    hops = STEPS * SPAN
    tiles = column_tiles(sites)
    me = lax.axis_index("tm")

    def at(offset):
        return {"tm": lax.rem(me + (offset % slices), slices)}

    spin_reach = min(hops, slices)
    log_reach = [SPAN * (STEPS - 1 - s) % slices for s in range(STEPS)]
    log_dist = sorted({d for d in log_reach if d != 0})

    fetch = pltpu.make_async_copy(start_ref, now, start_sem)
    fetch.start()

    targets = set(range(1, spin_reach)) | {slices - d for d in log_dist}
    greeted = sorted(targets | {slices - d for d in targets})
    barrier = pltpu.get_barrier_semaphore()
    for offset in greeted:
        pl.semaphore_signal(barrier, inc=1, device_id=at(offset), device_id_type=MESH)
    spins_all[0] = spins_ref[...]

    chunk = rows // 3

    def build(c, carry):
        first = pl.multiple_of(c * chunk, chunk)
        label = lax.broadcasted_iota(jnp.int32, (chunk, sites), 0) + first
        hit = table_ref[0:1, :] == label
        for k in range(1, 4):
            hit = hit | (table_ref[k:k + 1, :] == label)
        value = jnp.where(hit, DTAU, 0.0)
        bonds[pl.ds(first, chunk), :] = value.astype(jnp.bfloat16)
        bonds8[pl.ds(first, chunk), :] = value.astype(bonds8.dtype)
        return carry

    lax.fori_loop(0, sites // chunk, build, 0)

    pl.semaphore_wait(barrier, len(greeted))
    sends = []
    for d in range(1, spin_reach):
        copy = pltpu.make_async_remote_copy(
            src_ref=spins_all.at[0], dst_ref=spins_all.at[d],
            send_sem=spin_send.at[d], recv_sem=spin_recv.at[d],
            device_id=at(d), device_id_type=MESH,
        )
        copy.start()
        sends.append(copy)

    def square(c, carry):
        first = pl.multiple_of(c * rows, rows)
        block = pl.ds(first, rows)
        for lo, width in tiles:
            twice = jnp.dot(bonds8[block, :], bonds8[:, lo:lo + width], preferred_element_type=jnp.float32)
            one = bonds[block, lo:lo + width].astype(jnp.float32)
            rest[block, lo:lo + width] = (one + 0.5 * twice).astype(jnp.bfloat16)
        return carry

    lax.fori_loop(0, sites // rows, square, 0)

    fetch.wait()
    held[0] = now[...].astype(jnp.bfloat16)
    now[...] = held[0].astype(jnp.float32)

    for copy in sends:
        copy.wait()
    factors[...] = jnp.exp(LAMBDA * spins_all[...].astype(jnp.float32))

    scale_row[...] = jnp.ones_like(scale_row)
    logs[...] = jnp.zeros_like(logs)
    ones = jnp.ones((8, 128), jnp.float32)

    def log_copy(i):
        return pltpu.make_async_remote_copy(
            src_ref=logs.at[1 + i], dst_ref=landed.at[i],
            send_sem=log_send.at[i], recv_sem=log_recv.at[i],
            device_id=at(slices - log_dist[i]), device_id_type=MESH,
        )

    def step(s, carry):
        for a in range(SPAN):
            behind = lax.rem(hops - 1 - SPAN * s - a, slices)
            factor = factors.at[behind]
            last = a == SPAN - 1
            for lo, width in tiles:
                moved = jnp.dot(held[a % 2], rest[:, lo:lo + width], preferred_element_type=jnp.float32)
                value = (now[:, lo:lo + width] + moved) * factor[:, lo:lo + width]
                now[:, lo:lo + width] = value
                held[(a + 1) % 2, :, lo:lo + width] = value.astype(jnp.bfloat16)
                if last:
                    part = value * value
                    total = part[:, :128]
                    for q in range(128, width, 128):
                        total = total + part[:, q:q + 128]
                    squares[...] = total if lo == 0 else squares[...] + total
        summed = lax.dot_general(
            ones, squares[...], (((1,), (1,)), ((), ())),
            precision=lax.Precision.HIGHEST, preferred_element_type=jnp.float32,
        )
        scale = scale_row[...]
        rms = jnp.sqrt(summed * (1.0 / sites) * scale * scale + EPS)
        scale_row[...] = scale / rms
        gained = jnp.log(rms)
        for t in range(STEPS):
            slot = 0 if log_reach[t] == 0 else 1 + log_dist.index(log_reach[t])

            @pl.when(s == t)
            def _(slot=slot, t=t):
                logs[slot] = logs[slot] + gained
                if slot and all(log_reach[u] != log_reach[t] for u in range(t + 1, STEPS)):
                    log_copy(slot - 1).start()

        return carry

    lax.fori_loop(0, STEPS, step, 0)

    sign = 1.0
    for s in range(STEPS):
        slice_at = lax.rem(me + (slices - log_reach[s]) % slices, slices)
        sign = sign * jnp.where(slice_at < 4, -1.0, 1.0)
    pick = jnp.where(lax.broadcasted_iota(jnp.int32, (8, 128), 0) == 0, 1.0, 0.0)
    scale = lax.dot_general(
        scale_row[...], pick, (((0,), (0,)), ((), ())),
        precision=lax.Precision.HIGHEST, preferred_element_type=jnp.float32,
    ) * sign
    for lo in range(0, sites, 128):
        panels_ref[:, lo:lo + 128] = now[:, lo:lo + 128] * scale

    total = logs[0]
    for i in range(len(log_dist)):
        log_copy(i).wait()
        total = total + landed[i]
    growth_ref[...] = total[0:1] * (1.0 / (SPAN * STEPS))


def shards(slices, spins, neighbours, start):
    rows, sites = start.shape
    hops = STEPS * SPAN
    shift = hops % slices
    if shift:
        moved = lax.ppermute(
            start.astype(jnp.bfloat16), "tm", [(i, (i + shift) % slices) for i in range(slices)]
        )
        start = moved.astype(jnp.float32)
    reach = min(hops, slices)
    ways = max(1, len({SPAN * s % slices for s in range(1, STEPS)} - {0}))
    vmem = pl.BlockSpec(memory_space=pltpu.VMEM)
    panels, growth = pl.pallas_call(
        functools.partial(kernel, slices),
        out_shape=(
            jax.ShapeDtypeStruct((rows, sites), jnp.float32),
            jax.ShapeDtypeStruct((1, rows), jnp.float32),
        ),
        in_specs=[vmem, vmem, pl.BlockSpec(memory_space=pl.ANY)],
        out_specs=(vmem, vmem),
        scratch_shapes=[
            pltpu.VMEM((reach, 1, sites), jnp.int32),
            pltpu.VMEM((reach, 1, sites), jnp.float32),
            pltpu.VMEM((sites, sites), jnp.bfloat16),
            pltpu.VMEM((sites, sites), jnp.float8_e4m3fn),
            pltpu.VMEM((sites, sites), jnp.bfloat16),
            pltpu.VMEM((rows, sites), jnp.float32),
            pltpu.VMEM((2, rows, sites), jnp.bfloat16),
            pltpu.VMEM((rows, 128), jnp.float32),
            pltpu.VMEM((1 + ways, 8, rows), jnp.float32),
            pltpu.VMEM((ways, 8, rows), jnp.float32),
            pltpu.VMEM((8, rows), jnp.float32),
            pltpu.SemaphoreType.DMA,
            pltpu.SemaphoreType.DMA((reach,)),
            pltpu.SemaphoreType.DMA((reach,)),
            pltpu.SemaphoreType.DMA((ways,)),
            pltpu.SemaphoreType.DMA((ways,)),
        ],
        compiler_params=pltpu.CompilerParams(
            collective_id=0, has_side_effects=True, vmem_limit_bytes=40 * 1024 * 1024
        ),
        cost_estimate=pl.CostEstimate(
            flops=2 * (hops * rows + sites) * sites * sites,
            bytes_accessed=8 * rows * sites, transcendentals=0,
        ),
    )(spins, neighbours.T, start)
    return panels, growth.reshape(rows)


def solution(mesh):
    return jax.shard_map(
        functools.partial(shards, mesh.shape["tm"]),
        mesh=mesh,
        in_specs=(P("tm", None), P(), P(("tm", "panel"), None)),
        out_specs=(P(("tm", "panel"), None), P(("tm", "panel"))),
        check_vma=False,
    )
```

```python
import functools

import jax
import jax.numpy as jnp
from jax import lax
from jax.experimental import pallas as pl
from jax.experimental.pallas import tpu as pltpu
from jax.sharding import PartitionSpec as P

STEPS = 4
SPAN = 4
DTAU = 0.0625
LAMBDA = 0.5
EPS = 1e-06
TILE = 256
MESH = pl.DeviceIdType.MESH


def column_tiles(sites):
    return [(at, min(TILE, sites - at)) for at in range(0, sites, TILE)]


def kernel(
    slices, spins_ref, table_ref, start_ref, panels_ref, growth_ref,
    spins_all, table, factors, bonds, bonds8, rest, now, held, squares, logs, landed, scale_row,
    fetch_sem, store_sem, spin_send, spin_recv, log_send, log_recv,
):
    rows, sites = now.shape
    hops = STEPS * SPAN
    tiles = column_tiles(sites)
    me = lax.axis_index("tm")

    def at(offset):
        return {"tm": lax.rem(me + (offset % slices), slices)}

    spin_reach = min(hops, slices)
    log_reach = [SPAN * (STEPS - 1 - s) % slices for s in range(STEPS)]
    log_dist = sorted({d for d in log_reach if d != 0})

    fetch_table = pltpu.make_async_copy(table_ref, table, fetch_sem.at[0])
    fetch_spins = pltpu.make_async_copy(spins_ref, spins_all.at[0], fetch_sem.at[1])
    fetch = pltpu.make_async_copy(start_ref, now, fetch_sem.at[2])
    fetch_table.start()
    fetch_spins.start()
    fetch.start()

    targets = set(range(1, spin_reach)) | {slices - d for d in log_dist}
    greeted = sorted(targets | {slices - d for d in targets})
    barrier = pltpu.get_barrier_semaphore()
    for offset in greeted:
        pl.semaphore_signal(barrier, inc=1, device_id=at(offset), device_id_type=MESH)
    fetch_table.wait()

    chunk = rows // 3

    def build(c, carry):
        first = pl.multiple_of(c * chunk, chunk)
        label = lax.broadcasted_iota(jnp.int32, (chunk, sites), 0) + first
        hit = table[0:1, :] == label
        for k in range(1, 4):
            hit = hit | (table[k:k + 1, :] == label)
        value = jnp.where(hit, DTAU, 0.0)
        bonds[pl.ds(first, chunk), :] = value.astype(jnp.bfloat16)
        bonds8[pl.ds(first, chunk), :] = value.astype(bonds8.dtype)
        return carry

    lax.fori_loop(0, sites // chunk, build, 0)

    fetch_spins.wait()
    pl.semaphore_wait(barrier, len(greeted))
    sends = []
    for d in range(1, spin_reach):
        copy = pltpu.make_async_remote_copy(
            src_ref=spins_all.at[0], dst_ref=spins_all.at[d],
            send_sem=spin_send.at[d], recv_sem=spin_recv.at[d],
            device_id=at(d), device_id_type=MESH,
        )
        copy.start()
        sends.append(copy)

    def square(c, carry):
        first = pl.multiple_of(c * rows, rows)
        block = pl.ds(first, rows)
        for lo, width in tiles:
            twice = jnp.dot(bonds8[block, :], bonds8[:, lo:lo + width], preferred_element_type=jnp.float32)
            one = bonds[block, lo:lo + width].astype(jnp.float32)
            rest[block, lo:lo + width] = (one + 0.5 * twice).astype(jnp.bfloat16)
        return carry

    lax.fori_loop(0, sites // rows, square, 0)

    fetch.wait()
    held[0] = now[...].astype(jnp.bfloat16)
    now[...] = held[0].astype(jnp.float32)

    for copy in sends:
        copy.wait()
    factors[...] = jnp.exp(LAMBDA * spins_all[...].astype(jnp.float32))

    scale_row[...] = jnp.ones_like(scale_row)
    logs[...] = jnp.zeros_like(logs)
    def log_copy(i):
        return pltpu.make_async_remote_copy(
            src_ref=logs.at[1 + i], dst_ref=landed.at[i],
            send_sem=log_send.at[i], recv_sem=log_recv.at[i],
            device_id=at(slices - log_dist[i]), device_id_type=MESH,
        )

    def advance(s):
        for a in range(SPAN):
            factor = factors.at[lax.rem(hops - 1 - SPAN * s - a, slices)]
            last = a == SPAN - 1
            for lo, width in tiles:
                moved = jnp.dot(held[a % 2], rest[:, lo:lo + width], preferred_element_type=jnp.float32)
                value = (now[:, lo:lo + width] + moved) * factor[:, lo:lo + width]
                now[:, lo:lo + width] = value
                held[(a + 1) % 2, :, lo:lo + width] = value.astype(jnp.bfloat16)
                if last:
                    part = value * value
                    total = part[:, :128]
                    for q in range(128, width, 128):
                        total = total + part[:, q:q + 128]
                    squares[...] = total if lo == 0 else squares[...] + total

    def row_sums(values):
        high = values.astype(jnp.bfloat16)
        low = (values - high.astype(jnp.float32)).astype(jnp.bfloat16)
        ones = jnp.ones((16, 128), jnp.bfloat16)
        over = (((1,), (1,)), ((), ()))
        return (
            lax.dot_general(ones, high, over, preferred_element_type=jnp.float32)
            + lax.dot_general(ones, low, over, preferred_element_type=jnp.float32)
        )[:8]

    def account(s):
        scale = scale_row[...]
        rms = jnp.sqrt(row_sums(squares[...]) * (1.0 / sites) * scale * scale + EPS)
        scale_row[...] = scale / rms
        gained = jnp.log(rms)
        for slot in range(1 + len(log_dist)):
            distance = 0 if slot == 0 else log_dist[slot - 1]
            steps_of = [t for t in range(STEPS) if log_reach[t] == distance]
            if isinstance(s, int):
                if s in steps_of:
                    logs[slot] = logs[slot] + gained
            else:
                member = functools.reduce(jnp.logical_or, [s == t for t in steps_of])
                logs[slot] = logs[slot] + jnp.where(member, gained, 0.0)

    advance(0)

    def step(s, carry):
        account(s - 1)
        advance(s)
        return carry

    lax.fori_loop(1, STEPS - 1, step, 0)
    account(STEPS - 2)
    for i in range(len(log_dist)):
        log_copy(i).start()
    advance(STEPS - 1)
    account(STEPS - 1)

    sign = 1.0
    for s in range(STEPS):
        slice_at = lax.rem(me + (slices - log_reach[s]) % slices, slices)
        sign = sign * jnp.where(slice_at < 4, -1.0, 1.0)
    pick = jnp.where(lax.broadcasted_iota(jnp.int32, (8, 128), 0) == 0, 1.0, 0.0)
    scale = lax.dot_general(
        scale_row[...], pick, (((0,), (0,)), ((), ())),
        precision=lax.Precision.HIGHEST, preferred_element_type=jnp.float32,
    ) * sign
    parts = []
    for c in range(3):
        part = pl.ds(c * chunk, chunk)
        for lo in range(0, sites, 128):
            now[part, lo:lo + 128] = now[part, lo:lo + 128] * scale[c * chunk:(c + 1) * chunk]
        parts.append(pltpu.make_async_copy(now.at[part], panels_ref.at[part], store_sem.at[c]))
        parts[-1].start()

    total = logs[0]
    for i in range(len(log_dist)):
        log_copy(i).wait()
        total = total + landed[i]
    growth_ref[...] = total[0:1] * (1.0 / (SPAN * STEPS))
    for part in parts:
        part.wait()


def shards(slices, spins, neighbours, start):
    rows, sites = start.shape
    hops = STEPS * SPAN
    shift = hops % slices
    if shift:
        moved = lax.ppermute(
            start.astype(jnp.bfloat16), "tm", [(i, (i + shift) % slices) for i in range(slices)]
        )
        start = moved.astype(jnp.float32)
    reach = min(hops, slices)
    ways = max(1, len({SPAN * s % slices for s in range(1, STEPS)} - {0}))
    vmem = pl.BlockSpec(memory_space=pltpu.VMEM)
    panels, growth = pl.pallas_call(
        functools.partial(kernel, slices),
        out_shape=(
            jax.ShapeDtypeStruct((rows, sites), jnp.float32),
            jax.ShapeDtypeStruct((1, rows), jnp.float32),
        ),
        in_specs=[pl.BlockSpec(memory_space=pltpu.HBM)] * 3,
        out_specs=(pl.BlockSpec(memory_space=pltpu.HBM), vmem),
        scratch_shapes=[
            pltpu.VMEM((reach, 1, sites), jnp.int32),
            pltpu.VMEM((4, sites), jnp.int32),
            pltpu.VMEM((reach, 1, sites), jnp.float32),
            pltpu.VMEM((sites, sites), jnp.bfloat16),
            pltpu.VMEM((sites, sites), jnp.float8_e4m3fn),
            pltpu.VMEM((sites, sites), jnp.bfloat16),
            pltpu.VMEM((rows, sites), jnp.float32),
            pltpu.VMEM((2, rows, sites), jnp.bfloat16),
            pltpu.VMEM((rows, 128), jnp.float32),
            pltpu.VMEM((1 + ways, 8, rows), jnp.float32),
            pltpu.VMEM((ways, 8, rows), jnp.float32),
            pltpu.VMEM((8, rows), jnp.float32),
            pltpu.SemaphoreType.DMA((3,)),
            pltpu.SemaphoreType.DMA((3,)),
            pltpu.SemaphoreType.DMA((reach,)),
            pltpu.SemaphoreType.DMA((reach,)),
            pltpu.SemaphoreType.DMA((ways,)),
            pltpu.SemaphoreType.DMA((ways,)),
        ],
        compiler_params=pltpu.CompilerParams(
            collective_id=0, has_side_effects=True, vmem_limit_bytes=64 * 1024 * 1024
        ),
        cost_estimate=pl.CostEstimate(
            flops=2 * (hops * rows + sites) * sites * sites,
            bytes_accessed=8 * rows * sites, transcendentals=0,
        ),
    )(spins, neighbours.T, start)
    return panels, growth.reshape(rows)


def solution(mesh):
    return jax.shard_map(
        functools.partial(shards, mesh.shape["tm"]),
        mesh=mesh,
        in_specs=(P("tm", None), P(), P(("tm", "panel"), None)),
        out_specs=(P(("tm", "panel"), None), P(("tm", "panel"))),
        check_vma=False,
    )
```

```python
import functools

import jax
import jax.numpy as jnp
from jax import lax
from jax.experimental import pallas as pl
from jax.experimental.pallas import tpu as pltpu
from jax.sharding import PartitionSpec as P

STEPS = 4
SPAN = 4
DTAU = 0.0625
LAMBDA = 0.5
EPS = 1e-06
TILE = 1152
MESH = pl.DeviceIdType.MESH


def column_tiles(sites):
    return [(at, min(TILE, sites - at)) for at in range(0, sites, TILE)]


def kernel(
    slices, table, start_ref, panels_ref, growth_ref,
    spins_all, factors, bonds, bonds8, rest, now, held, squares, logs, landed, scale_row,
    fetch_sem, spin_send, spin_recv, log_send, log_recv,
):
    rows, sites = now.shape
    hops = STEPS * SPAN
    tiles = column_tiles(sites)
    me = lax.axis_index("tm")

    def at(offset):
        return {"tm": lax.rem(me + (offset % slices), slices)}

    spin_reach = min(hops, slices)
    log_reach = [SPAN * (STEPS - 1 - s) % slices for s in range(STEPS)]
    log_dist = sorted({d for d in log_reach if d != 0})

    fetch = pltpu.make_async_copy(start_ref, now, fetch_sem)
    fetch.start()

    targets = set(range(1, spin_reach)) | {slices - d for d in log_dist}
    greeted = sorted(targets | {slices - d for d in targets})
    barrier = pltpu.get_barrier_semaphore()
    for offset in greeted:
        pl.semaphore_signal(barrier, inc=1, device_id=at(offset), device_id_type=MESH)
    spins_all[0] = table[4:5, :]

    chunk = rows // 3

    def build(c, carry):
        first = pl.multiple_of(c * chunk, chunk)
        label = lax.broadcasted_iota(jnp.int32, (chunk, sites), 0) + first
        hit = table[0:1, :] == label
        for k in range(1, 4):
            hit = hit | (table[k:k + 1, :] == label)
        value = jnp.where(hit, DTAU, 0.0)
        bonds[pl.ds(first, chunk), :] = value.astype(jnp.bfloat16)
        bonds8[pl.ds(first, chunk), :] = value.astype(bonds8.dtype)
        return carry

    lax.fori_loop(0, sites // chunk, build, 0)

    pl.semaphore_wait(barrier, len(greeted))
    sends = []
    for d in range(1, spin_reach):
        copy = pltpu.make_async_remote_copy(
            src_ref=spins_all.at[0], dst_ref=spins_all.at[d],
            send_sem=spin_send.at[d], recv_sem=spin_recv.at[d],
            device_id=at(d), device_id_type=MESH,
        )
        copy.start()
        sends.append(copy)

    def square(c, carry):
        first = pl.multiple_of(c * rows, rows)
        block = pl.ds(first, rows)
        for lo, width in tiles:
            twice = jnp.dot(bonds8[block, :], bonds8[:, lo:lo + width], preferred_element_type=jnp.float32)
            one = bonds[block, lo:lo + width].astype(jnp.float32)
            rest[block, lo:lo + width] = (one + 0.5 * twice).astype(jnp.bfloat16)
        return carry

    lax.fori_loop(0, sites // rows, square, 0)

    fetch.wait()
    held[0] = now[...].astype(jnp.bfloat16)
    now[...] = held[0].astype(jnp.float32)

    for copy in sends:
        copy.wait()
    factors[...] = jnp.exp(LAMBDA * spins_all[...].astype(jnp.float32))

    scale_row[...] = jnp.ones_like(scale_row)
    logs[...] = jnp.zeros_like(logs)
    def log_copy(i):
        return pltpu.make_async_remote_copy(
            src_ref=logs.at[1 + i], dst_ref=landed.at[i],
            send_sem=log_send.at[i], recv_sem=log_recv.at[i],
            device_id=at(slices - log_dist[i]), device_id_type=MESH,
        )

    def advance(s):
        for a in range(SPAN):
            factor = factors.at[lax.rem(hops - 1 - SPAN * s - a, slices)]
            last = a == SPAN - 1
            for lo, width in tiles:
                moved = jnp.dot(held[a % 2], rest[:, lo:lo + width], preferred_element_type=jnp.float32)
                value = (now[:, lo:lo + width] + moved) * factor[:, lo:lo + width]
                now[:, lo:lo + width] = value
                held[(a + 1) % 2, :, lo:lo + width] = value.astype(jnp.bfloat16)
                if last:
                    part = value * value
                    total = part[:, :128]
                    for q in range(128, width, 128):
                        total = total + part[:, q:q + 128]
                    squares[...] = total if lo == 0 else squares[...] + total

    def row_sums(values):
        high = values.astype(jnp.bfloat16)
        low = (values - high.astype(jnp.float32)).astype(jnp.bfloat16)
        ones = jnp.ones((16, 128), jnp.bfloat16)
        over = (((1,), (1,)), ((), ()))
        return (
            lax.dot_general(ones, high, over, preferred_element_type=jnp.float32)
            + lax.dot_general(ones, low, over, preferred_element_type=jnp.float32)
        )[:8]

    def account(s):
        scale = scale_row[...]
        rms = jnp.sqrt(row_sums(squares[...]) * (1.0 / sites) * scale * scale + EPS)
        scale_row[...] = scale / rms
        gained = jnp.log(rms)
        for slot in range(1 + len(log_dist)):
            distance = 0 if slot == 0 else log_dist[slot - 1]
            steps_of = [t for t in range(STEPS) if log_reach[t] == distance]
            if isinstance(s, int):
                if s in steps_of:
                    logs[slot] = logs[slot] + gained
            else:
                member = functools.reduce(jnp.logical_or, [s == t for t in steps_of])
                logs[slot] = logs[slot] + jnp.where(member, gained, 0.0)

    advance(0)

    def step(s, carry):
        account(s - 1)
        advance(s)
        return carry

    lax.fori_loop(1, STEPS - 1, step, 0)
    account(STEPS - 2)
    for i in range(len(log_dist)):
        log_copy(i).start()
    advance(STEPS - 1)
    account(STEPS - 1)

    sign = 1.0
    for s in range(STEPS):
        slice_at = lax.rem(me + (slices - log_reach[s]) % slices, slices)
        sign = sign * jnp.where(slice_at < 4, -1.0, 1.0)
    pick = jnp.where(lax.broadcasted_iota(jnp.int32, (8, 128), 0) == 0, 1.0, 0.0)
    scale = lax.dot_general(
        scale_row[...], pick, (((0,), (0,)), ((), ())),
        precision=lax.Precision.HIGHEST, preferred_element_type=jnp.float32,
    ) * sign
    for lo in range(0, sites, 128):
        panels_ref[:, lo:lo + 128] = now[:, lo:lo + 128] * scale

    total = logs[0]
    for i in range(len(log_dist)):
        log_copy(i).wait()
        total = total + landed[i]
    growth_ref[...] = total[0:1] * (1.0 / (SPAN * STEPS))


def shards(slices, spins, neighbours, start):
    rows, sites = start.shape
    hops = STEPS * SPAN
    shift = hops % slices
    if shift:
        moved = lax.ppermute(
            start.astype(jnp.bfloat16), "tm", [(i, (i + shift) % slices) for i in range(slices)]
        )
        start = moved.astype(jnp.float32)
    reach = min(hops, slices)
    ways = max(1, len({SPAN * s % slices for s in range(1, STEPS)} - {0}))
    vmem = pl.BlockSpec(memory_space=pltpu.VMEM)
    panels, growth = pl.pallas_call(
        functools.partial(kernel, slices),
        out_shape=(
            jax.ShapeDtypeStruct((rows, sites), jnp.float32),
            jax.ShapeDtypeStruct((1, rows), jnp.float32),
        ),
        in_specs=[vmem, pl.BlockSpec(memory_space=pl.ANY)],
        out_specs=(vmem, vmem),
        scratch_shapes=[
            pltpu.VMEM((reach, 1, sites), jnp.int32),
            pltpu.VMEM((reach, 1, sites), jnp.float32),
            pltpu.VMEM((sites, sites), jnp.bfloat16),
            pltpu.VMEM((sites, sites), jnp.float8_e4m3fn),
            pltpu.VMEM((sites, sites), jnp.bfloat16),
            pltpu.VMEM((rows, sites), jnp.float32),
            pltpu.VMEM((2, rows, sites), jnp.bfloat16),
            pltpu.VMEM((rows, 128), jnp.float32),
            pltpu.VMEM((1 + ways, 8, rows), jnp.float32),
            pltpu.VMEM((ways, 8, rows), jnp.float32),
            pltpu.VMEM((8, rows), jnp.float32),
            pltpu.SemaphoreType.DMA,
            pltpu.SemaphoreType.DMA((reach,)),
            pltpu.SemaphoreType.DMA((reach,)),
            pltpu.SemaphoreType.DMA((ways,)),
            pltpu.SemaphoreType.DMA((ways,)),
        ],
        compiler_params=pltpu.CompilerParams(
            collective_id=0, has_side_effects=True, vmem_limit_bytes=52 * 1024 * 1024
        ),
        cost_estimate=pl.CostEstimate(
            flops=2 * (hops * rows + sites) * sites * sites,
            bytes_accessed=8 * rows * sites, transcendentals=0,
        ),
    )(jnp.concatenate([neighbours.T, spins], axis=0), start)
    return panels, growth.reshape(rows)


def solution(mesh):
    return jax.shard_map(
        functools.partial(shards, mesh.shape["tm"]),
        mesh=mesh,
        in_specs=(P("tm", None), P(), P(("tm", "panel"), None)),
        out_specs=(P(("tm", "panel"), None), P(("tm", "panel"))),
        check_vma=False,
    )
```

```python
import functools

import jax
import jax.numpy as jnp
from jax import lax
from jax.experimental import pallas as pl
from jax.experimental.pallas import tpu as pltpu
from jax.sharding import PartitionSpec as P

STEPS = 4
SPAN = 4
DTAU = 0.0625
LAMBDA = 0.5
EPS = 1e-06
TILE = 1152
COARSE = 8
LEVEL = 0.0625
CARRY = 1.1276
MESH = pl.DeviceIdType.MESH


def column_tiles(sites):
    return [(at, min(TILE, sites - at)) for at in range(0, sites, TILE)]


def kernel(
    slices, table, start_ref, panels_ref, growth_ref,
    spins_all, factors, bonds, bonds8, rest, rest8, now, held, held8, owed, squares, logs, landed, scale_row,
    fetch_sem, spin_send, spin_recv, log_send, log_recv,
):
    rows, sites = now.shape
    hops = STEPS * SPAN
    tiles = column_tiles(sites)
    me = lax.axis_index("tm")

    def at(offset):
        return {"tm": lax.rem(me + (offset % slices), slices)}

    spin_reach = min(hops, slices)
    log_reach = [SPAN * (STEPS - 1 - s) % slices for s in range(STEPS)]
    log_dist = sorted({d for d in log_reach if d != 0})

    fetch = pltpu.make_async_copy(start_ref, now, fetch_sem)
    fetch.start()

    targets = set(range(1, spin_reach)) | {slices - d for d in log_dist}
    greeted = sorted(targets | {slices - d for d in targets})
    barrier = pltpu.get_barrier_semaphore()
    for offset in greeted:
        pl.semaphore_signal(barrier, inc=1, device_id=at(offset), device_id_type=MESH)
    spins_all[0] = table[4:5, :]

    chunk = rows // 3

    def build(c, carry):
        first = pl.multiple_of(c * chunk, chunk)
        label = lax.broadcasted_iota(jnp.int32, (chunk, sites), 0) + first
        hit = table[0:1, :] == label
        for k in range(1, 4):
            hit = hit | (table[k:k + 1, :] == label)
        value = jnp.where(hit, DTAU, 0.0)
        bonds[pl.ds(first, chunk), :] = value.astype(jnp.bfloat16)
        bonds8[pl.ds(first, chunk), :] = value.astype(bonds8.dtype)
        return carry

    lax.fori_loop(0, sites // chunk, build, 0)

    pl.semaphore_wait(barrier, len(greeted))
    sends = []
    for d in range(1, spin_reach):
        copy = pltpu.make_async_remote_copy(
            src_ref=spins_all.at[0], dst_ref=spins_all.at[d],
            send_sem=spin_send.at[d], recv_sem=spin_recv.at[d],
            device_id=at(d), device_id_type=MESH,
        )
        copy.start()
        sends.append(copy)

    def row_sums(values):
        high = values.astype(jnp.bfloat16)
        low = (values - high.astype(jnp.float32)).astype(jnp.bfloat16)
        ones = jnp.ones((16, 128), jnp.bfloat16)
        over = (((1,), (1,)), ((), ()))
        return (
            lax.dot_general(ones, high, over, preferred_element_type=jnp.float32)
            + lax.dot_general(ones, low, over, preferred_element_type=jnp.float32)
        )[:8]

    def to_column(line):
        pick = jnp.where(lax.broadcasted_iota(jnp.int32, (8, 128), 0) == 0, 1.0, 0.0)
        return lax.dot_general(
            line, pick, (((0,), (0,)), ((), ())),
            precision=lax.Precision.HIGHEST, preferred_element_type=jnp.float32,
        )

    def square(c, carry):
        first = pl.multiple_of(c * rows, rows)
        block = pl.ds(first, rows)
        for lo, width in tiles:
            twice = jnp.dot(bonds8[block, :], bonds8[:, lo:lo + width], preferred_element_type=jnp.float32)
            one = bonds[block, lo:lo + width].astype(jnp.float32)
            both = one + 0.5 * twice
            rest[block, lo:lo + width] = both.astype(jnp.bfloat16)
            rest8[block, lo:lo + width] = (both * 512.0).astype(rest8.dtype)
        return carry

    lax.fori_loop(0, sites // rows, square, 0)

    fetch.wait()
    for lo in range(0, sites, 128):
        value = now[:, lo:lo + 128].astype(jnp.bfloat16).astype(jnp.float32)
        now[:, lo:lo + 128] = value
        squares[...] = value * value if lo == 0 else squares[...] + value * value
    level = jnp.sqrt(row_sums(squares[...]) * (1.0 / sites) + 1e-30) * (1.0 / LEVEL)
    scale_row[...] = level
    scale = to_column(1.0 / level)
    for lo in range(0, sites, 128):
        value = now[:, lo:lo + 128] * scale
        now[:, lo:lo + 128] = value
        eighth = value.astype(held8.dtype)
        held8[0, :, lo:lo + 128] = eighth
        owed[:, lo:lo + 128] = (value - eighth.astype(jnp.float32)) * CARRY

    for copy in sends:
        copy.wait()
    factors[...] = jnp.exp(LAMBDA * spins_all[...].astype(jnp.float32))

    logs[...] = jnp.zeros_like(logs)
    def log_copy(i):
        return pltpu.make_async_remote_copy(
            src_ref=logs.at[1 + i], dst_ref=landed.at[i],
            send_sem=log_send.at[i], recv_sem=log_recv.at[i],
            device_id=at(slices - log_dist[i]), device_id_type=MESH,
        )

    def advance(s, coarse):
        for a in range(SPAN):
            factor = factors.at[lax.rem(hops - 1 - SPAN * s - a, slices)]
            last = a == SPAN - 1
            for lo, width in tiles:
                span = slice(lo, lo + width)
                if coarse:
                    moved = jnp.dot(held8[a % 2], rest8[:, span], preferred_element_type=jnp.float32) * (1.0 / 512.0)
                else:
                    moved = jnp.dot(held[a % 2], rest[:, span], preferred_element_type=jnp.float32)
                value = (now[:, span] + moved) * factor[:, span]
                now[:, span] = value
                if coarse:
                    wanted = value + owed[:, span]
                    if last and (s + 1) * SPAN == COARSE:
                        held[0, :, span] = wanted.astype(jnp.bfloat16)
                    else:
                        eighth = wanted.astype(held8.dtype)
                        held8[(a + 1) % 2, :, span] = eighth
                        owed[:, span] = (wanted - eighth.astype(jnp.float32)) * CARRY
                else:
                    held[(a + 1) % 2, :, span] = value.astype(jnp.bfloat16)
                if last:
                    part = value * value
                    total = part[:, :128]
                    for q in range(128, width, 128):
                        total = total + part[:, q:q + 128]
                    squares[...] = total if lo == 0 else squares[...] + total

    def account(s):
        scale = scale_row[...]
        rms = jnp.sqrt(row_sums(squares[...]) * (1.0 / sites) * scale * scale + EPS)
        scale_row[...] = scale / rms
        gained = jnp.log(rms)
        for slot in range(1 + len(log_dist)):
            distance = 0 if slot == 0 else log_dist[slot - 1]
            steps_of = [t for t in range(STEPS) if log_reach[t] == distance]
            if s in steps_of:
                logs[slot] = logs[slot] + gained

    for s in range(STEPS):
        advance(s, s * SPAN < COARSE)
        account(s)
        if s == STEPS - 2:
            for i in range(len(log_dist)):
                log_copy(i).start()

    sign = 1.0
    for s in range(STEPS):
        slice_at = lax.rem(me + (slices - log_reach[s]) % slices, slices)
        sign = sign * jnp.where(slice_at < 4, -1.0, 1.0)
    scale = to_column(scale_row[...]) * sign
    for lo in range(0, sites, 128):
        panels_ref[:, lo:lo + 128] = now[:, lo:lo + 128] * scale

    total = logs[0]
    for i in range(len(log_dist)):
        log_copy(i).wait()
        total = total + landed[i]
    growth_ref[...] = total[0:1] * (1.0 / (SPAN * STEPS))


def shards(slices, spins, neighbours, start):
    rows, sites = start.shape
    hops = STEPS * SPAN
    shift = hops % slices
    if shift:
        moved = lax.ppermute(
            start.astype(jnp.bfloat16), "tm", [(i, (i + shift) % slices) for i in range(slices)]
        )
        start = moved.astype(jnp.float32)
    reach = min(hops, slices)
    ways = max(1, len({SPAN * s % slices for s in range(1, STEPS)} - {0}))
    vmem = pl.BlockSpec(memory_space=pltpu.VMEM)
    panels, growth = pl.pallas_call(
        functools.partial(kernel, slices),
        out_shape=(
            jax.ShapeDtypeStruct((rows, sites), jnp.float32),
            jax.ShapeDtypeStruct((1, rows), jnp.float32),
        ),
        in_specs=[vmem, pl.BlockSpec(memory_space=pl.ANY)],
        out_specs=(vmem, vmem),
        scratch_shapes=[
            pltpu.VMEM((reach, 1, sites), jnp.int32),
            pltpu.VMEM((reach, 1, sites), jnp.float32),
            pltpu.VMEM((sites, sites), jnp.bfloat16),
            pltpu.VMEM((sites, sites), jnp.float8_e4m3fn),
            pltpu.VMEM((sites, sites), jnp.bfloat16),
            pltpu.VMEM((sites, sites), jnp.float8_e4m3fn),
            pltpu.VMEM((rows, sites), jnp.float32),
            pltpu.VMEM((2, rows, sites), jnp.bfloat16),
            pltpu.VMEM((2, rows, sites), jnp.float8_e4m3fn),
            pltpu.VMEM((rows, sites), jnp.float32),
            pltpu.VMEM((rows, 128), jnp.float32),
            pltpu.VMEM((1 + ways, 8, rows), jnp.float32),
            pltpu.VMEM((ways, 8, rows), jnp.float32),
            pltpu.VMEM((8, rows), jnp.float32),
            pltpu.SemaphoreType.DMA,
            pltpu.SemaphoreType.DMA((reach,)),
            pltpu.SemaphoreType.DMA((reach,)),
            pltpu.SemaphoreType.DMA((ways,)),
            pltpu.SemaphoreType.DMA((ways,)),
        ],
        compiler_params=pltpu.CompilerParams(
            collective_id=0, has_side_effects=True, vmem_limit_bytes=52 * 1024 * 1024
        ),
        cost_estimate=pl.CostEstimate(
            flops=2 * (hops * rows + sites) * sites * sites,
            bytes_accessed=8 * rows * sites, transcendentals=0,
        ),
    )(jnp.concatenate([neighbours.T, spins], axis=0), start)
    return panels, growth.reshape(rows)


def solution(mesh):
    return jax.shard_map(
        functools.partial(shards, mesh.shape["tm"]),
        mesh=mesh,
        in_specs=(P("tm", None), P(), P(("tm", "panel"), None)),
        out_specs=(P(("tm", "panel"), None), P(("tm", "panel"))),
        check_vma=False,
    )
```

```python
import functools

import jax
import jax.numpy as jnp
from jax import lax
from jax.experimental import pallas as pl
from jax.experimental.pallas import tpu as pltpu
from jax.sharding import PartitionSpec as P

STEPS = 4
SPAN = 4
DTAU = 0.0625
LAMBDA = 0.5
EPS = 1e-06
TILE = 1152
COARSE = 15
LEVEL = 0.0625
LEVEL_LATER = 0.015625
CARRY = 1.1276
MESH = pl.DeviceIdType.MESH


def column_tiles(sites):
    return [(at, min(TILE, sites - at)) for at in range(0, sites, TILE)]


def kernel(
    slices, table, start_ref, panels_ref, growth_ref,
    spins_all, factors, bonds, bonds8, rest, rest8, now, held, held8, owed, squares, logs, landed, scale_row, level_row,
    fetch_sem, spin_send, spin_recv, log_send, log_recv,
):
    rows, sites = now.shape
    hops = STEPS * SPAN
    tiles = column_tiles(sites)
    me = lax.axis_index("tm")

    def at(offset):
        return {"tm": lax.rem(me + (offset % slices), slices)}

    spin_reach = min(hops, slices)
    log_reach = [SPAN * (STEPS - 1 - s) % slices for s in range(STEPS)]
    log_dist = sorted({d for d in log_reach if d != 0})

    fetch = pltpu.make_async_copy(start_ref, now, fetch_sem)
    fetch.start()

    targets = set(range(1, spin_reach)) | {slices - d for d in log_dist}
    greeted = sorted(targets | {slices - d for d in targets})
    barrier = pltpu.get_barrier_semaphore()
    for offset in greeted:
        pl.semaphore_signal(barrier, inc=1, device_id=at(offset), device_id_type=MESH)
    spins_all[0] = table[4:5, :]

    chunk = rows // 3

    def build(c, carry):
        first = pl.multiple_of(c * chunk, chunk)
        label = lax.broadcasted_iota(jnp.int32, (chunk, sites), 0) + first
        hit = table[0:1, :] == label
        for k in range(1, 4):
            hit = hit | (table[k:k + 1, :] == label)
        value = jnp.where(hit, DTAU, 0.0)
        bonds[pl.ds(first, chunk), :] = value.astype(jnp.bfloat16)
        bonds8[pl.ds(first, chunk), :] = value.astype(bonds8.dtype)
        return carry

    lax.fori_loop(0, sites // chunk, build, 0)

    pl.semaphore_wait(barrier, len(greeted))
    sends = []
    for d in range(1, spin_reach):
        copy = pltpu.make_async_remote_copy(
            src_ref=spins_all.at[0], dst_ref=spins_all.at[d],
            send_sem=spin_send.at[d], recv_sem=spin_recv.at[d],
            device_id=at(d), device_id_type=MESH,
        )
        copy.start()
        sends.append(copy)

    def row_sums(values):
        high = values.astype(jnp.bfloat16)
        low = (values - high.astype(jnp.float32)).astype(jnp.bfloat16)
        ones = jnp.ones((16, 128), jnp.bfloat16)
        over = (((1,), (1,)), ((), ()))
        return (
            lax.dot_general(ones, high, over, preferred_element_type=jnp.float32)
            + lax.dot_general(ones, low, over, preferred_element_type=jnp.float32)
        )[:8]

    def to_column(line):
        pick = jnp.where(lax.broadcasted_iota(jnp.int32, (8, 128), 0) == 0, 1.0, 0.0)
        return lax.dot_general(
            line, pick, (((0,), (0,)), ((), ())),
            precision=lax.Precision.HIGHEST, preferred_element_type=jnp.float32,
        )

    def square(c, carry):
        first = pl.multiple_of(c * rows, rows)
        block = pl.ds(first, rows)
        for lo, width in tiles:
            twice = jnp.dot(bonds8[block, :], bonds8[:, lo:lo + width], preferred_element_type=jnp.float32)
            one = bonds[block, lo:lo + width].astype(jnp.float32)
            both = one + 0.5 * twice
            rest[block, lo:lo + width] = both.astype(jnp.bfloat16)
            rest8[block, lo:lo + width] = (both * 512.0).astype(rest8.dtype)
        return carry

    lax.fori_loop(0, sites // rows, square, 0)

    fetch.wait()
    for lo in range(0, sites, 128):
        value = now[:, lo:lo + 128].astype(jnp.bfloat16).astype(jnp.float32)
        now[:, lo:lo + 128] = value
        squares[...] = value * value if lo == 0 else squares[...] + value * value
    level = jnp.sqrt(row_sums(squares[...]) * (1.0 / sites) + 1e-30) * (1.0 / LEVEL)
    scale_row[...] = level
    scale = to_column(1.0 / level)
    for lo in range(0, sites, 128):
        value = now[:, lo:lo + 128] * scale
        now[:, lo:lo + 128] = value
        eighth = value.astype(held8.dtype)
        held8[0, :, lo:lo + 128] = eighth
        owed[:, lo:lo + 128] = (value - eighth.astype(jnp.float32)) * CARRY

    for copy in sends:
        copy.wait()
    factors[...] = jnp.exp(LAMBDA * spins_all[...].astype(jnp.float32))

    logs[...] = jnp.zeros_like(logs)
    def log_copy(i):
        return pltpu.make_async_remote_copy(
            src_ref=logs.at[1 + i], dst_ref=landed.at[i],
            send_sem=log_send.at[i], recv_sem=log_recv.at[i],
            device_id=at(slices - log_dist[i]), device_id_type=MESH,
        )

    def advance(s):
        for a in range(SPAN):
            hop = s * SPAN + a
            coarse, coarse_next = hop < COARSE, hop + 1 < COARSE
            factor = factors.at[lax.rem(hops - 1 - hop, slices)]
            last = a == SPAN - 1
            rescale = last and s == 1
            if rescale:
                column = to_column(level_row[...])
                scale_row[...] = scale_row[...] / level_row[...]
            for lo, width in tiles:
                span = slice(lo, lo + width)
                if coarse:
                    moved = jnp.dot(held8[hop % 2], rest8[:, span], preferred_element_type=jnp.float32) * (1.0 / 512.0)
                else:
                    moved = jnp.dot(held[hop % 2], rest[:, span], preferred_element_type=jnp.float32)
                value = (now[:, span] + moved) * factor[:, span]
                debt = owed[:, span] if coarse else None
                if rescale:
                    wide = jnp.concatenate([column] * (width // 128), axis=1)
                    value = value * wide
                    debt = debt * wide
                now[:, span] = value
                wanted = value + debt if coarse else value
                if coarse_next:
                    eighth = wanted.astype(held8.dtype)
                    held8[(hop + 1) % 2, :, span] = eighth
                    owed[:, span] = (wanted - eighth.astype(jnp.float32)) * CARRY
                elif hop + 1 < hops:
                    held[(hop + 1) % 2, :, span] = wanted.astype(jnp.bfloat16)
                if last:
                    part = value * value
                    total = part[:, :128]
                    for q in range(128, width, 128):
                        total = total + part[:, q:q + 128]
                    squares[...] = total if lo == 0 else squares[...] + total

    def account(s):
        scale = scale_row[...]
        power = row_sums(squares[...]) * (1.0 / sites)
        if s == 0:
            level_row[...] = LEVEL_LATER / jnp.sqrt(power + 1e-30)
        rms = jnp.sqrt(power * scale * scale + EPS)
        scale_row[...] = scale / rms
        gained = jnp.log(rms)
        for slot in range(1 + len(log_dist)):
            distance = 0 if slot == 0 else log_dist[slot - 1]
            steps_of = [t for t in range(STEPS) if log_reach[t] == distance]
            if s in steps_of:
                logs[slot] = logs[slot] + gained

    for s in range(STEPS):
        advance(s)
        account(s)
        if s == STEPS - 2:
            for i in range(len(log_dist)):
                log_copy(i).start()

    sign = 1.0
    for s in range(STEPS):
        slice_at = lax.rem(me + (slices - log_reach[s]) % slices, slices)
        sign = sign * jnp.where(slice_at < 4, -1.0, 1.0)
    scale = to_column(scale_row[...]) * sign
    for lo in range(0, sites, 128):
        panels_ref[:, lo:lo + 128] = now[:, lo:lo + 128] * scale

    total = logs[0]
    for i in range(len(log_dist)):
        log_copy(i).wait()
        total = total + landed[i]
    growth_ref[...] = total[0:1] * (1.0 / (SPAN * STEPS))


def shards(slices, spins, neighbours, start):
    rows, sites = start.shape
    hops = STEPS * SPAN
    shift = hops % slices
    if shift:
        moved = lax.ppermute(
            start.astype(jnp.bfloat16), "tm", [(i, (i + shift) % slices) for i in range(slices)]
        )
        start = moved.astype(jnp.float32)
    reach = min(hops, slices)
    ways = max(1, len({SPAN * s % slices for s in range(1, STEPS)} - {0}))
    vmem = pl.BlockSpec(memory_space=pltpu.VMEM)
    panels, growth = pl.pallas_call(
        functools.partial(kernel, slices),
        out_shape=(
            jax.ShapeDtypeStruct((rows, sites), jnp.float32),
            jax.ShapeDtypeStruct((1, rows), jnp.float32),
        ),
        in_specs=[vmem, pl.BlockSpec(memory_space=pl.ANY)],
        out_specs=(vmem, vmem),
        scratch_shapes=[
            pltpu.VMEM((reach, 1, sites), jnp.int32),
            pltpu.VMEM((reach, 1, sites), jnp.float32),
            pltpu.VMEM((sites, sites), jnp.bfloat16),
            pltpu.VMEM((sites, sites), jnp.float8_e4m3fn),
            pltpu.VMEM((sites, sites), jnp.bfloat16),
            pltpu.VMEM((sites, sites), jnp.float8_e4m3fn),
            pltpu.VMEM((rows, sites), jnp.float32),
            pltpu.VMEM((2, rows, sites), jnp.bfloat16),
            pltpu.VMEM((2, rows, sites), jnp.float8_e4m3fn),
            pltpu.VMEM((rows, sites), jnp.float32),
            pltpu.VMEM((rows, 128), jnp.float32),
            pltpu.VMEM((1 + ways, 8, rows), jnp.float32),
            pltpu.VMEM((ways, 8, rows), jnp.float32),
            pltpu.VMEM((8, rows), jnp.float32),
            pltpu.VMEM((8, rows), jnp.float32),
            pltpu.SemaphoreType.DMA,
            pltpu.SemaphoreType.DMA((reach,)),
            pltpu.SemaphoreType.DMA((reach,)),
            pltpu.SemaphoreType.DMA((ways,)),
            pltpu.SemaphoreType.DMA((ways,)),
        ],
        compiler_params=pltpu.CompilerParams(
            collective_id=0, has_side_effects=True, vmem_limit_bytes=52 * 1024 * 1024
        ),
        cost_estimate=pl.CostEstimate(
            flops=2 * (hops * rows + sites) * sites * sites,
            bytes_accessed=8 * rows * sites, transcendentals=0,
        ),
    )(jnp.concatenate([neighbours.T, spins], axis=0), start)
    return panels, growth.reshape(rows)


def solution(mesh):
    return jax.shard_map(
        functools.partial(shards, mesh.shape["tm"]),
        mesh=mesh,
        in_specs=(P("tm", None), P(), P(("tm", "panel"), None)),
        out_specs=(P(("tm", "panel"), None), P(("tm", "panel"))),
        check_vma=False,
    )
```

```python
import functools

import jax
import jax.numpy as jnp
from jax import lax
from jax.experimental import pallas as pl
from jax.experimental.pallas import tpu as pltpu
from jax.sharding import PartitionSpec as P

STEPS = 4
SPAN = 4
DTAU = 0.0625
LAMBDA = 0.5
EPS = 1e-06
TILE = 1152
COARSE = 15
LEVEL = 0.0625
LEVEL_LATER = 0.015625
CARRY = 1.1276
MESH = pl.DeviceIdType.MESH


def column_tiles(sites):
    return [(at, min(TILE, sites - at)) for at in range(0, sites, TILE)]


def kernel(
    slices, table, start_ref, panels_ref, growth_ref,
    spins_all, factors, bonds, bonds8, rest, rest8, now, held, held8, owed, squares, logs, landed, scale_row, level_row,
    fetch_sem, spin_send, spin_recv, log_send, log_recv,
):
    rows, sites = now.shape
    hops = STEPS * SPAN
    tiles = column_tiles(sites)
    me = lax.axis_index("tm")

    def at(offset):
        return {"tm": lax.rem(me + (offset % slices), slices)}

    spin_reach = min(hops, slices)
    log_reach = [SPAN * (STEPS - 1 - s) % slices for s in range(STEPS)]
    log_dist = sorted({d for d in log_reach if d != 0})

    fetch = pltpu.make_async_copy(start_ref, now, fetch_sem)
    fetch.start()

    targets = set(range(1, spin_reach)) | {slices - d for d in log_dist}
    greeted = sorted(targets | {slices - d for d in targets})
    barrier = pltpu.get_barrier_semaphore()
    for offset in greeted:
        pl.semaphore_signal(barrier, inc=1, device_id=at(offset), device_id_type=MESH)
    spins_all[0] = table[4:5, :]

    chunk = rows // 3

    def build(c, carry):
        first = pl.multiple_of(c * chunk, chunk)
        label = lax.broadcasted_iota(jnp.int32, (chunk, sites), 0) + first
        hit = table[0:1, :] == label
        for k in range(1, 4):
            hit = hit | (table[k:k + 1, :] == label)
        value = jnp.where(hit, DTAU, 0.0)
        bonds[pl.ds(first, chunk), :] = value.astype(jnp.bfloat16)
        bonds8[pl.ds(first, chunk), :] = value.astype(bonds8.dtype)
        return carry

    lax.fori_loop(0, sites // chunk, build, 0)

    pl.semaphore_wait(barrier, len(greeted))
    sends = []
    for d in range(1, spin_reach):
        copy = pltpu.make_async_remote_copy(
            src_ref=spins_all.at[0], dst_ref=spins_all.at[d],
            send_sem=spin_send.at[d], recv_sem=spin_recv.at[d],
            device_id=at(d), device_id_type=MESH,
        )
        copy.start()
        sends.append(copy)

    def row_sums(values):
        high = values.astype(jnp.bfloat16)
        low = (values - high.astype(jnp.float32)).astype(jnp.bfloat16)
        ones = jnp.ones((16, 128), jnp.bfloat16)
        over = (((1,), (1,)), ((), ()))
        return (
            lax.dot_general(ones, high, over, preferred_element_type=jnp.float32)
            + lax.dot_general(ones, low, over, preferred_element_type=jnp.float32)
        )[:8]

    def to_column(line):
        pick = jnp.where(lax.broadcasted_iota(jnp.int32, (8, 128), 0) == 0, 1.0, 0.0)
        return lax.dot_general(
            line, pick, (((0,), (0,)), ((), ())),
            precision=lax.Precision.HIGHEST, preferred_element_type=jnp.float32,
        )

    def square(c, carry):
        first = pl.multiple_of(c * rows, rows)
        block = pl.ds(first, rows)
        for lo, width in tiles:
            twice = jnp.dot(bonds8[block, :], bonds8[:, lo:lo + width], preferred_element_type=jnp.float32)
            one = bonds[block, lo:lo + width].astype(jnp.float32)
            both = one + 0.5 * twice
            rest[block, lo:lo + width] = both.astype(jnp.bfloat16)
            rest8[block, lo:lo + width] = (both * 512.0).astype(rest8.dtype)
        return carry

    lax.fori_loop(0, sites // rows, square, 0)

    fetch.wait()
    for lo in range(0, sites, 128):
        value = now[:, lo:lo + 128].astype(jnp.bfloat16).astype(jnp.float32)
        now[:, lo:lo + 128] = value
        squares[...] = value * value if lo == 0 else squares[...] + value * value
    level = jnp.sqrt(row_sums(squares[...]) * (1.0 / sites) + 1e-30) * (1.0 / LEVEL)
    scale_row[...] = level
    scale = to_column(1.0 / level)
    for lo in range(0, sites, 128):
        value = now[:, lo:lo + 128] * scale
        now[:, lo:lo + 128] = value
        eighth = value.astype(held8.dtype)
        held8[0, :, lo:lo + 128] = eighth
        owed[:, lo:lo + 128] = ((value - eighth.astype(jnp.float32)) * CARRY).astype(owed.dtype)

    for copy in sends:
        copy.wait()
    factors[...] = jnp.exp(LAMBDA * spins_all[...].astype(jnp.float32))

    logs[...] = jnp.zeros_like(logs)
    def log_copy(i):
        return pltpu.make_async_remote_copy(
            src_ref=logs.at[1 + i], dst_ref=landed.at[i],
            send_sem=log_send.at[i], recv_sem=log_recv.at[i],
            device_id=at(slices - log_dist[i]), device_id_type=MESH,
        )

    def advance(s):
        for a in range(SPAN):
            hop = s * SPAN + a
            coarse, coarse_next = hop < COARSE, hop + 1 < COARSE
            factor = factors.at[lax.rem(hops - 1 - hop, slices)]
            last = a == SPAN - 1
            rescale = last and s == 1
            if rescale:
                column = to_column(level_row[...])
                scale_row[...] = scale_row[...] / level_row[...]
            for lo, width in tiles:
                span = slice(lo, lo + width)
                if coarse:
                    moved = jnp.dot(held8[hop % 2], rest8[:, span], preferred_element_type=jnp.float32) * (1.0 / 512.0)
                else:
                    moved = jnp.dot(held[hop % 2], rest[:, span], preferred_element_type=jnp.float32)
                value = (now[:, span] + moved) * factor[:, span]
                debt = owed[:, span].astype(jnp.float32) if coarse else None
                if rescale:
                    wide = jnp.concatenate([column] * (width // 128), axis=1)
                    value = value * wide
                    debt = debt * wide
                now[:, span] = value
                wanted = value + debt if coarse else value
                if coarse_next:
                    eighth = wanted.astype(held8.dtype)
                    held8[(hop + 1) % 2, :, span] = eighth
                    owed[:, span] = ((wanted - eighth.astype(jnp.float32)) * CARRY).astype(owed.dtype)
                elif hop + 1 < hops:
                    held[(hop + 1) % 2, :, span] = wanted.astype(jnp.bfloat16)
                if last:
                    part = value * value
                    total = part[:, :128]
                    for q in range(128, width, 128):
                        total = total + part[:, q:q + 128]
                    squares[...] = total if lo == 0 else squares[...] + total

    def account(s):
        scale = scale_row[...]
        power = row_sums(squares[...]) * (1.0 / sites)
        if s == 0:
            level_row[...] = LEVEL_LATER / jnp.sqrt(power + 1e-30)
        rms = jnp.sqrt(power * scale * scale + EPS)
        scale_row[...] = scale / rms
        gained = jnp.log(rms)
        for slot in range(1 + len(log_dist)):
            distance = 0 if slot == 0 else log_dist[slot - 1]
            steps_of = [t for t in range(STEPS) if log_reach[t] == distance]
            if s in steps_of:
                logs[slot] = logs[slot] + gained

    for s in range(STEPS):
        advance(s)
        account(s)
        if s == STEPS - 2:
            for i in range(len(log_dist)):
                log_copy(i).start()

    sign = 1.0
    for s in range(STEPS):
        slice_at = lax.rem(me + (slices - log_reach[s]) % slices, slices)
        sign = sign * jnp.where(slice_at < 4, -1.0, 1.0)
    scale = to_column(scale_row[...]) * sign
    for lo in range(0, sites, 128):
        panels_ref[:, lo:lo + 128] = now[:, lo:lo + 128] * scale

    total = logs[0]
    for i in range(len(log_dist)):
        log_copy(i).wait()
        total = total + landed[i]
    growth_ref[...] = total[0:1] * (1.0 / (SPAN * STEPS))


def shards(slices, spins, neighbours, start):
    rows, sites = start.shape
    hops = STEPS * SPAN
    shift = hops % slices
    if shift:
        moved = lax.ppermute(
            start.astype(jnp.bfloat16), "tm", [(i, (i + shift) % slices) for i in range(slices)]
        )
        start = moved.astype(jnp.float32)
    reach = min(hops, slices)
    ways = max(1, len({SPAN * s % slices for s in range(1, STEPS)} - {0}))
    vmem = pl.BlockSpec(memory_space=pltpu.VMEM)
    panels, growth = pl.pallas_call(
        functools.partial(kernel, slices),
        out_shape=(
            jax.ShapeDtypeStruct((rows, sites), jnp.float32),
            jax.ShapeDtypeStruct((1, rows), jnp.float32),
        ),
        in_specs=[vmem, pl.BlockSpec(memory_space=pl.ANY)],
        out_specs=(vmem, vmem),
        scratch_shapes=[
            pltpu.VMEM((reach, 1, sites), jnp.int32),
            pltpu.VMEM((reach, 1, sites), jnp.float32),
            pltpu.VMEM((sites, sites), jnp.bfloat16),
            pltpu.VMEM((sites, sites), jnp.float8_e4m3fn),
            pltpu.VMEM((sites, sites), jnp.bfloat16),
            pltpu.VMEM((sites, sites), jnp.float8_e4m3fn),
            pltpu.VMEM((rows, sites), jnp.float32),
            pltpu.VMEM((2, rows, sites), jnp.bfloat16),
            pltpu.VMEM((2, rows, sites), jnp.float8_e4m3fn),
            pltpu.VMEM((rows, sites), jnp.bfloat16),
            pltpu.VMEM((rows, 128), jnp.float32),
            pltpu.VMEM((1 + ways, 8, rows), jnp.float32),
            pltpu.VMEM((ways, 8, rows), jnp.float32),
            pltpu.VMEM((8, rows), jnp.float32),
            pltpu.VMEM((8, rows), jnp.float32),
            pltpu.SemaphoreType.DMA,
            pltpu.SemaphoreType.DMA((reach,)),
            pltpu.SemaphoreType.DMA((reach,)),
            pltpu.SemaphoreType.DMA((ways,)),
            pltpu.SemaphoreType.DMA((ways,)),
        ],
        compiler_params=pltpu.CompilerParams(
            collective_id=0, has_side_effects=True, vmem_limit_bytes=52 * 1024 * 1024
        ),
        cost_estimate=pl.CostEstimate(
            flops=2 * (hops * rows + sites) * sites * sites,
            bytes_accessed=8 * rows * sites, transcendentals=0,
        ),
    )(jnp.concatenate([neighbours.T, spins], axis=0), start)
    return panels, growth.reshape(rows)


def solution(mesh):
    return jax.shard_map(
        functools.partial(shards, mesh.shape["tm"]),
        mesh=mesh,
        in_specs=(P("tm", None), P(), P(("tm", "panel"), None)),
        out_specs=(P(("tm", "panel"), None), P(("tm", "panel"))),
        check_vma=False,
    )
```
